32 devices in a mesh: row: 4 (over x, core), col: 8 (over z, y).
Axes of the slice: x: 2, y: 2, z: 4, core: 2. Of those that a mesh axis runs over, the one named last changes fastest.
Arguments:
- features: bfloat16 [16384, 256], P('row'), may hold values from -6 to 6
- join_weight: bfloat16 [256, 256], replicated, may hold values from -0.375 to 0.375
- partner: int32 [16384], replicated, may hold values from 0 to 16383, as said below
- tile_index: int32 [3328], P(('row', 'col')), may hold values from 0 to 127, as said below
- tile_values: bfloat16 [3328, 256, 256], P(('row', 'col')), may hold values from 0 to 10
- pert_slot: int32 [128], P(('row', 'col')), may hold values from 0 to 103
- pert_values: bfloat16 [128, 256, 256], P(('row', 'col')), may hold values from 0 to 0.5
- routes: int32 [3328, 5], P(('row', 'col')), may hold values from 0 to 31, as said below
Outputs:
- coarse_features: bfloat16 [8192, 256], P('row')
- coarse_quarters: bfloat16 [5120, 128, 128], P(('row', 'col'))
The draws below stay inside these ranges and needn't reach their ends.
Inputs may be any that keep to these rules, and one draw needn't show every extreme that they name: `partner`: fine nodes 8192 + k * 256 + j and k * 256 + s are partners of each other, where s runs over a permutation of the 256 slots for each coarse tile k. `tile_index`: each entry is a local tile position i * 8 + j with i below 16; the entries of one device are distinct; the four devices whose row indices agree modulo 4 // 2 and whose col indices agree modulo 8 // 2 hold the same list in the same order. `routes`: every column of a row equals column 0. Among the 104 rows of one device no device number appears more than 5 times, and in every draw some device number appears exactly 5 times among one device's rows.
All inputs are finite; a program needn't handle non-finite values.
Results may differ from the reference program's by a relative error of at most 0.0052.
Values may be sent and summed in bfloat16 or wider, within the bound.
A program may use at most 192 MiB of HBM per device.

```python
import math
import jax
import jax.numpy as jnp
from jax import lax

TILE = 256
FEAT = 256
TC = 8
NZ = 104
NP = 4
CAP = 5
TR = 16
NT = 64
N = 16384
NCT = 32
NC = 8192
N_ROW = 4
N_COL = 8
DEVICES = 32


def group_lists(key):
    count = N_ROW // 2 * (N_COL // 2)
    subkeys = jax.random.split(jax.random.fold_in(key, 11), count)
    slot_lists = jax.vmap(lambda subkey: jax.random.permutation(subkey, TR * TC)[:NZ])(subkeys)
    slot_lists = slot_lists.reshape(N_ROW // 2, N_COL // 2, NZ).astype(jnp.int32)
    return jnp.tile(slot_lists, (2, 2, 1))


def draw_tile_index(key, part):
    return group_lists(key).reshape(-1).astype(jnp.int32)


def draw_tile_values(key, part):
    position_list = group_lists(key)
    low_log = math.log(0.35)
    high_log = math.log(2.8)
    floor_value = 0.1
    row_factor = jnp.exp(jax.random.uniform(jax.random.fold_in(key, 12), (N, N_COL), jnp.float32, low_log, high_log))
    col_factor = jnp.exp(jax.random.uniform(jax.random.fold_in(key, 14), (N, N_ROW), jnp.float32, low_log, high_log))
    row_ids = jnp.arange(N_ROW, dtype=jnp.int32)[:, None, None]
    col_ids = jnp.arange(N_COL, dtype=jnp.int32)[None, :, None]
    row_tiles = row_ids * TR + position_list // TC
    col_tiles = col_ids * TC + position_list % TC
    offsets = jnp.arange(TILE, dtype=jnp.int32)
    row_nodes = row_tiles[..., None] * TILE + offsets
    col_nodes = col_tiles[..., None] * TILE + offsets
    row_scale = row_factor[row_nodes, col_ids[..., None]]
    col_scale = col_factor[col_nodes, row_ids[..., None]]
    noise = jax.random.uniform(jax.random.fold_in(key, 13), (N_ROW, N_COL, NZ, TILE, TILE), jnp.float32, floor_value, 1.0)
    result = jnp.minimum(noise * row_scale[..., :, None] * col_scale[..., None, :], 10.0)
    return result.reshape(N_ROW * N_COL * NZ, TILE, TILE).astype(jnp.bfloat16)


def draw_partner(key, part):
    subkeys = jax.random.split(jax.random.fold_in(key, 21), NCT)
    slot_perms = jax.vmap(lambda subkey: jax.random.permutation(subkey, TILE))(subkeys).astype(jnp.int32)
    inverse = jnp.argsort(slot_perms, axis=1).astype(jnp.int32)
    tile_start = (jnp.arange(NCT, dtype=jnp.int32) * TILE)[:, None]
    first_half = NC + tile_start + inverse
    second_half = tile_start + slot_perms
    return jnp.concatenate([first_half.reshape(-1), second_half.reshape(-1)]).astype(jnp.int32)


def device_routes(subkey):
    devices = N_ROW * N_COL
    base_key = jax.random.fold_in(subkey, 1)
    busy = jax.random.randint(jax.random.fold_in(subkey, 2), (), 0, devices).astype(jnp.int32)
    weights = jax.random.randint(base_key, (devices,), 1, 64).astype(jnp.int32)
    weights = weights * weights
    slot_pool = jnp.repeat(jnp.arange(devices, dtype=jnp.int32), CAP, total_repeat_length=devices * CAP)
    pool_weight = jnp.repeat(weights, CAP, total_repeat_length=devices * CAP)
    within = jnp.tile(jnp.arange(CAP, dtype=jnp.int32), devices)
    noise = jax.random.randint(jax.random.fold_in(subkey, 3), (devices * CAP,), 0, 4096).astype(jnp.int32)
    score = pool_weight * 4096 + noise
    score = jnp.where(slot_pool == busy, 2 ** 30 - within, score)
    score = score * (devices * CAP) + jnp.arange(devices * CAP, dtype=jnp.int32)
    order = jnp.argsort(-score, stable=True)[:NZ]
    picked = slot_pool[order]
    shuffle = jax.random.permutation(jax.random.fold_in(subkey, 4), NZ)
    return picked[shuffle].astype(jnp.int32)


def draw_routes(key, part):
    devices = N_ROW * N_COL
    subkeys = jax.random.split(jax.random.fold_in(key, 31), devices)
    targets = jax.vmap(device_routes)(subkeys).reshape(-1)
    return jnp.broadcast_to(targets[:, None], (devices * NZ, CAP)).astype(jnp.int32)


def plant(values, rng, smallest, top_value):
    extent = values.shape
    spot = [jax.random.randint(jax.random.fold_in(rng, axis), (), 0, extent[axis]) for axis in range(len(extent))]
    values = values.at[tuple(spot)].set(smallest)
    longest = extent.index(max(extent))
    spot[longest] = (spot[longest] + 1) % extent[longest]
    return values.at[tuple(spot)].set(top_value)


def levels(key, extent, cuts, smallest, top_value):
    level, own = 1.0, jax.random.fold_in(key, 6)
    for dim, parts in cuts:
        heights = jnp.exp(jax.random.uniform(jax.random.fold_in(own, dim), (parts,), jnp.float32, smallest / len(cuts), top_value / len(cuts)))
        level = level * jnp.repeat(heights, extent[dim] // parts).reshape([-1 if axis == dim else 1 for axis in range(len(extent))])
    return level


def centred(own_key, shape, spread, most, cuts=(), held_as=jnp.bfloat16):
    values = jax.random.normal(own_key, shape, jnp.float32) * spread
    if len(cuts) > 0:
        values = levels(own_key, shape, cuts, -0.22, 0.18) * values
    return jnp.clip(values, min=-most, max=most).astype(held_as)


def setup_inputs(seed: int = 0) -> dict:
    key_of = jax.random.split(jax.random.key(seed), 9)
    features = centred(key_of[0], (N, FEAT), 1.0, 6.0, ((0, 4),))
    join_weight = centred(key_of[1], (FEAT, FEAT), FEAT ** -0.5, 0.375)
    partner = draw_partner(jax.random.fold_in(key_of[8], 71), 0)
    tile_index = draw_tile_index(jax.random.fold_in(key_of[8], 71), 0)
    tile_values = draw_tile_values(jax.random.fold_in(key_of[8], 71), 0)
    pert_slot = plant(jax.random.randint(key_of[5], (DEVICES * NP,), 0, NZ), jax.random.fold_in(key_of[5], 1), 0, NZ - 1).astype(jnp.int32)
    pert_values = jnp.clip(0.5 * jax.random.uniform(key_of[6], (DEVICES * NP, TILE, TILE), jnp.float32) ** levels(key_of[6], (DEVICES * NP, TILE, TILE), ((0, 32),), -0.2, 0.2), 0.0, 0.5).astype(jnp.bfloat16)
    routes = draw_routes(jax.random.fold_in(key_of[8], 71), 0)
    return dict(features=features, join_weight=join_weight, partner=partner, tile_index=tile_index, tile_values=tile_values, pert_slot=pert_slot, pert_values=pert_values, routes=routes)


def group_pairing(partner):
    odd_slots = partner[NC:].reshape(NCT, TILE) - (jnp.arange(NCT, dtype=jnp.int32) * TILE)[:, None]
    return jnp.argsort(odd_slots, axis=1).astype(jnp.int32)

def reference(features, join_weight, partner, tile_index, tile_values, pert_slot, pert_values, routes):
    half_tile = TILE // 2
    row_half = N_ROW // 2
    col_half = N_COL // 2
    groups = row_half * col_half
    inverse = group_pairing(partner)
    values = tile_values.reshape(N_ROW, N_COL, NZ, TILE, TILE)
    indices = tile_index.reshape(N_ROW, N_COL, NZ)
    extra_values = pert_values.reshape(N_ROW, N_COL, NP, TILE, TILE)
    extra_slots = pert_slot.reshape(N_ROW, N_COL, NP)

    def group_total(group_id):
        group_row = group_id // col_half
        group_col = group_id % col_half
        coarse_total = jnp.zeros((NZ, TILE, TILE), jnp.float32)
        for side_row in range(2):
            for side_col in range(2):
                row_pos = side_row * row_half + group_row
                col_pos = side_col * col_half + group_col
                tile_block = values[row_pos, col_pos].astype(jnp.float32)
                tile_block = tile_block.at[extra_slots[row_pos, col_pos]].add(extra_values[row_pos, col_pos].astype(jnp.float32))
                tile_block = tile_block.astype(jnp.bfloat16)
                local_tiles = indices[row_pos, col_pos]
                coarse_row = group_row * TR + local_tiles // TC
                coarse_col = group_col * TC + local_tiles % TC
                if side_row == 1:
                    row_pick = jnp.broadcast_to(inverse[coarse_row][:, :, None], tile_block.shape)
                    tile_block = jnp.take_along_axis(tile_block, row_pick, axis=1)
                if side_col == 1:
                    col_pick = jnp.broadcast_to(inverse[coarse_col][:, None, :], tile_block.shape)
                    tile_block = jnp.take_along_axis(tile_block, col_pick, axis=2)
                coarse_total = coarse_total + tile_block.astype(jnp.float32)
        local_tiles = indices[group_row, group_col]
        return (coarse_total, group_row * TR + local_tiles // TC, group_col * TC + local_tiles % TC)

    def group_sums(group_id):
        coarse_total, coarse_row, coarse_col = group_total(group_id)
        return (lax.optimization_barrier(jnp.sum(coarse_total, axis=2)), coarse_row)
    group_ids = jnp.arange(groups, dtype=jnp.int32)
    row_sums, row_tiles = lax.map(group_sums, group_ids)
    summed = jnp.zeros((NCT, TILE), jnp.float32).at[row_tiles.reshape(-1)].add(row_sums.reshape(-1, TILE))
    degree = 1.0 + summed / NC

    def group_quarters(group_id):
        coarse_total, coarse_row, coarse_col = group_total(group_id)
        pieces = []
        for side_row in range(2):
            for side_col in range(2):
                row_deg = degree[coarse_row][:, side_row * half_tile:(side_row + 1) * half_tile]
                col_deg = degree[coarse_col][:, side_col * half_tile:(side_col + 1) * half_tile]
                quarter = coarse_total[:, side_row * half_tile:(side_row + 1) * half_tile, side_col * half_tile:(side_col + 1) * half_tile]
                pieces.append((quarter / jnp.sqrt(row_deg[:, :, None] * col_deg[:, None, :])).astype(jnp.bfloat16))
        return jnp.stack(pieces).reshape(2, 2, NZ, half_tile, half_tile)
    quarters = lax.map(group_quarters, group_ids)
    targets = routes[:, 0].reshape(N_ROW * N_COL, NZ)
    slot_order = jnp.arange(NZ, dtype=jnp.int32)
    earlier = lax.optimization_barrier(jnp.sum(((targets[:, :, None] == targets[:, None, :]) & (slot_order[None, None, :] < slot_order[None, :, None])).astype(jnp.int32), axis=2))
    sender = (jnp.arange(2, dtype=jnp.int32)[None, :, None] * row_half + (group_ids // col_half)[:, None, None]) * N_COL
    sender = sender + jnp.arange(2, dtype=jnp.int32)[None, None, :] * col_half + (group_ids % col_half)[:, None, None]
    sender = jnp.broadcast_to(sender[..., None], (groups, 2, 2, NZ)).astype(jnp.int32)
    slot_ids = jnp.broadcast_to(slot_order, (groups, 2, 2, NZ))
    receiver = targets[sender, slot_ids]
    position = sender * CAP + earlier[sender, slot_ids]
    delivered = jnp.zeros((N_ROW * N_COL, N_ROW * N_COL * CAP, half_tile, half_tile), jnp.bfloat16)
    delivered = delivered.at[receiver, position].set(quarters)
    coarse_quarters = delivered.reshape(-1, half_tile, half_tile)
    node_tiles = features.reshape(NT, TILE, FEAT)
    feat_pick = jnp.broadcast_to(inverse[:, :, None], (NCT, TILE, FEAT))
    second_half = jnp.take_along_axis(node_tiles[NCT:], feat_pick, axis=1)
    merged = (node_tiles[:NCT].astype(jnp.float32) + second_half.astype(jnp.float32)).astype(jnp.bfloat16)
    joined_rows = jnp.dot(merged.reshape(NC, FEAT), join_weight, preferred_element_type=jnp.float32).reshape(NCT, TILE, FEAT)
    scaled = (joined_rows / jnp.sqrt(degree)[:, :, None]).astype(jnp.bfloat16)
    coarse_features = scaled.reshape(NCT, 2, half_tile, FEAT).transpose(1, 0, 2, 3).reshape(NC, FEAT)
    return (coarse_features, coarse_quarters)
```

```python
import functools

import jax
import jax.numpy as jnp
from jax import lax
from jax.experimental import pallas as pl
from jax.experimental.pallas import tpu as pltpu
from jax.sharding import PartitionSpec as P

F32 = jnp.float32
BF16 = jnp.bfloat16
LAG = 3


def onehot(table_row, size):
    levels = lax.broadcasted_iota(jnp.int32, (size, size), 0)
    return (table_row == levels).astype(F32).astype(BF16)


def kernel(
    dims,
    row_slot, col_slot, pert_id, source, source_row, source_col,
    row_tab, col_tab, pert, weight, feats, tiles,
    feat_out, quarter_out,
    row_hot, col_hot, inbox, row_send, row_keep, row_recv, col_send, col_recv, quarter,
    feat_send, feat_keep, feat_recv, total, deg_recv, row_scale, col_scale, out_send,
    in_sem, row_ss, row_rs, col_ss, col_rs, feat_ss, feat_rs, deg_ss, deg_rs, out_ss, out_rs,
    own_sem,
):
    rows, cols, slots, size, tiles_row, tiles_col, cap, chunk, feat_chunk, coarse_nodes = dims
    half = size // 2
    devices = rows * cols
    chunks = slots // chunk
    feat_chunks = tiles_row // feat_chunk
    r = lax.axis_index("row")
    c = lax.axis_index("col")
    me = r * cols + c
    row_peer = (lax.rem(r + rows // 2, rows), c)
    col_peer = (r, lax.rem(c + cols // 2, cols))

    def fetch(k):
        return pltpu.make_async_copy(
            tiles.at[pl.ds(k * chunk, chunk)], inbox.at[lax.rem(k, 2)], in_sem.at[lax.rem(k, 2)]
        )

    def row_copy(k):
        part = pl.ds(k * chunk, chunk)
        return pltpu.make_async_remote_copy(
            src_ref=row_send.at[part], dst_ref=row_recv.at[part],
            send_sem=row_ss.at[k], recv_sem=row_rs.at[k],
            device_id=row_peer, device_id_type=pl.DeviceIdType.MESH,
        )

    def col_copy(k):
        part = pl.ds(k * chunk, chunk)
        return pltpu.make_async_remote_copy(
            src_ref=col_send.at[part], dst_ref=col_recv.at[part],
            send_sem=col_ss.at[k], recv_sem=col_rs.at[k],
            device_id=col_peer, device_id_type=pl.DeviceIdType.MESH,
        )

    def feat_copy(k):
        part = pl.ds(k * feat_chunk, feat_chunk)
        return pltpu.make_async_remote_copy(
            src_ref=feat_send.at[part], dst_ref=feat_recv.at[part],
            send_sem=feat_ss.at[k], recv_sem=feat_rs.at[k],
            device_id=row_peer, device_id_type=pl.DeviceIdType.MESH,
        )

    def deg_copy(peer, slot):
        return pltpu.make_async_remote_copy(
            src_ref=deg_recv.at[me], dst_ref=deg_recv.at[slot],
            send_sem=deg_ss.at[peer], recv_sem=deg_rs.at[slot],
            device_id=(peer // cols, lax.rem(peer, cols)),
            device_id_type=pl.DeviceIdType.MESH,
        )

    def out_copy(peer, slot):
        return pltpu.make_async_remote_copy(
            src_ref=out_send.at[pl.ds(peer * cap, cap)],
            dst_ref=quarter_out.at[pl.ds(slot * cap, cap)],
            send_sem=out_ss.at[peer], recv_sem=out_rs.at[slot],
            device_id=(peer // cols, lax.rem(peer, cols)),
            device_id_type=pl.DeviceIdType.MESH,
        )

    def over_peers(body):
        def step(k, carry):
            body(lax.rem(me + k, devices))
            return carry

        lax.fori_loop(1, devices, step, 0)

    fetch(0).start()
    barrier = pltpu.get_barrier_semaphore()

    def greet(peer):
        pl.semaphore_signal(
            barrier, inc=1, device_id=(peer // cols, lax.rem(peer, cols)),
            device_id_type=pl.DeviceIdType.MESH,
        )

    over_peers(greet)

    def build_row(i, carry):
        row_hot[i] = onehot(row_tab[i], size)
        return carry

    def build_col(i, carry):
        col_hot[i] = onehot(col_tab[i], size)
        return carry

    lax.fori_loop(0, tiles_row, build_row, 0)
    lax.fori_loop(0, tiles_col, build_col, 0)
    total[...] = jnp.zeros_like(total)
    quarter[slots] = jnp.zeros((half, half), F32)
    pl.semaphore_wait(barrier, devices - 1)

    def pair_tiles(k):
        @pl.when(k + 1 < chunks)
        def _():
            fetch(k + 1).start()

        fetch(k).wait()
        box = lax.rem(k, 2)
        keep = lax.rem(k, LAG + 1)
        for t in range(chunk):
            n = k * chunk + t
            tile = (inbox[box, t].astype(F32) + pert[pert_id[n]]).astype(BF16)
            paired = jnp.dot(
                row_hot[row_slot[n]], tile, preferred_element_type=F32
            ).astype(BF16)
            paired = lax.dot_general(
                paired, col_hot[col_slot[n]], (((1,), (1,)), ((), ())),
                preferred_element_type=F32,
            ).astype(BF16)
            row_send[n] = paired[:half]
            row_keep[keep, t] = paired[half:]
        row_copy(k).start()

    def pair_feats(k):
        def one(t, carry):
            n = k * feat_chunk + t
            paired = jnp.dot(row_hot[n], feats[n], preferred_element_type=F32).astype(BF16)
            feat_send[n] = paired[:half]
            feat_keep[n] = paired[half:]
            return carry

        lax.fori_loop(0, feat_chunk, one, 0)
        feat_copy(k).start()

    def sum_rows(k):
        row_copy(k).wait_recv()
        keep = lax.rem(k, LAG + 1)
        for t in range(chunk):
            n = k * chunk + t
            summed = row_keep[keep, t].astype(F32) + row_recv[n].astype(F32)
            col_send[n] = summed[:, :half].astype(BF16)
            quarter[n] = summed[:, half:]
        col_copy(k).start()

    def sum_cols(k):
        col_copy(k).wait_recv()
        lanes = lax.broadcasted_iota(jnp.int32, (half, 128), 1)
        for t in range(chunk):
            n = k * chunk + t
            value = quarter[n] + col_recv[n].astype(F32)
            quarter[n] = value
            sums = jnp.sum(value, axis=1, keepdims=True)
            total[...] += jnp.where(lanes == row_slot[n], sums, 0.0)

    def step(k, carry):
        pl.when(k < chunks)(lambda: pair_tiles(k))
        pl.when((k >= chunks) & (k < chunks + feat_chunks))(lambda: pair_feats(k - chunks))
        pl.when((k >= LAG) & (k < chunks + LAG))(lambda: sum_rows(k - LAG))
        pl.when((k >= 2 * LAG) & (k < chunks + 2 * LAG))(lambda: sum_cols(k - 2 * LAG))
        return carry

    lax.fori_loop(0, chunks + max(2 * LAG, feat_chunks), step, 0)

    deg_recv[me] = total[...].T[:tiles_row]
    over_peers(lambda peer: deg_copy(peer, me).start())
    over_peers(lambda peer: deg_copy(peer, peer).wait_recv())

    def inverse_root(row):
        def add(j, value):
            return value + deg_recv[row * cols + j]

        sums = lax.fori_loop(0, cols, add, jnp.zeros((tiles_row, half), F32))
        return 1.0 / jnp.sqrt(1.0 + sums / coarse_nodes)

    group_col = lax.rem(c, cols // 2) * tiles_col
    col_owner = c // (cols // 2) * (rows // 2) + group_col // tiles_row
    col_first = lax.rem(group_col, tiles_row)
    col_root = inverse_root(col_owner)
    row_root = inverse_root(r)
    row_root = jnp.concatenate([row_root, jnp.zeros((128 - tiles_row, half), F32)], axis=0).T
    for i in range(tiles_row):
        col_scale[i] = col_root[i : i + 1]
        row_scale[i] = jnp.broadcast_to(row_root[:, i : i + 1], (half, half))

    def fill(peer):
        for m in range(cap):
            t = peer * cap + m
            value = (
                quarter[source[t]] * row_scale[source_row[t]]
            ) * col_scale[source_col[t] + col_first]
            out_send[t] = value.astype(BF16)

    def send(peer):
        fill(peer)
        out_copy(peer, me).start()

    over_peers(send)
    fill(me)
    own = pltpu.make_async_copy(
        out_send.at[pl.ds(me * cap, cap)], quarter_out.at[pl.ds(me * cap, cap)], own_sem
    )
    own.start()

    def join(k, carry):
        feat_copy(k).wait_recv()

        def one(t, inner):
            n = k * feat_chunk + t
            merged = (feat_keep[n].astype(F32) + feat_recv[n].astype(F32)).astype(BF16)
            joined = jnp.dot(merged, weight[...], preferred_element_type=F32)
            feat_out[n] = (joined * row_scale[n][:, :1]).astype(BF16)
            return inner

        return lax.fori_loop(0, feat_chunk, one, carry)

    lax.fori_loop(0, feat_chunks, join, 0)

    def finish_pair(k, carry):
        row_copy(k).wait_send()
        col_copy(k).wait_send()
        return carry

    def finish_feat(k, carry):
        feat_copy(k).wait_send()
        return carry

    lax.fori_loop(0, chunks, finish_pair, 0)
    lax.fori_loop(0, feat_chunks, finish_feat, 0)
    over_peers(lambda peer: deg_copy(peer, me).wait_send())
    own.wait()
    over_peers(lambda peer: out_copy(peer, me).wait_send())
    over_peers(lambda peer: out_copy(peer, peer).wait_recv())


def local(features, join_weight, partner, tile_index, tile_values, pert_slot, pert_values, routes):
    rows = lax.axis_size("row")
    cols = lax.axis_size("col")
    row_half = rows // 2
    col_half = cols // 2
    row_index = lax.axis_index("row")
    col_index = lax.axis_index("col")
    row_side = row_index // row_half
    col_side = col_index // col_half
    slots, size, _ = tile_values.shape
    half = size // 2
    feat_width = features.shape[1]
    tiles_row = features.shape[0] // size
    node_tiles = partner.shape[0] // size
    tiles_col = node_tiles // cols
    coarse_count = node_tiles // 2
    coarse_nodes = coarse_count * size
    cap = routes.shape[1]
    pert_count = pert_slot.shape[0]
    devices = rows * cols
    chunk = next(n for n in (4, 2, 1) if slots % n == 0)
    feat_chunk = next(n for n in (4, 2, 1) if tiles_row % n == 0)
    chunks = slots // chunk
    feat_chunks = tiles_row // feat_chunk

    odd_slots = (
        partner[coarse_nodes:].reshape(coarse_count, size)
        - (jnp.arange(coarse_count, dtype=jnp.int32) * size)[:, None]
    )
    even_slots = jnp.arange(size, dtype=jnp.int32)[None, :]

    def table(start, count, side):
        part = lax.dynamic_slice_in_dim(odd_slots, start, count, 0)
        return (jnp.where(side == 1, part, even_slots) ^ (half * (1 - side)))[:, None, :]

    row_tab = table(row_index % row_half * tiles_row, tiles_row, row_side)
    col_tab = table(col_index % col_half * tiles_col, tiles_col, col_side)
    local_row = tile_index // tiles_col
    local_col = tile_index % tiles_col

    same = pert_slot[:, None] == pert_slot[None, :]
    pert_sum = jnp.sum(
        jnp.where(same[:, :, None, None], pert_values.astype(F32)[None], 0.0), axis=1
    )
    pert_sum = jnp.concatenate([pert_sum, jnp.zeros((1, size, size), F32)], axis=0)
    order = jnp.arange(slots, dtype=jnp.int32)
    pert_id = jnp.min(
        jnp.where(
            pert_slot[:, None] == order[None, :],
            jnp.arange(pert_count, dtype=jnp.int32)[:, None],
            pert_count,
        ),
        axis=0,
    )
    targets = routes[:, 0]
    earlier = jnp.sum(
        ((targets[:, None] == targets[None, :]) & (order[None, :] < order[:, None])).astype(
            jnp.int32
        ),
        axis=1,
    )
    position = targets * cap + earlier
    place = position[None, :] == jnp.arange(devices * cap, dtype=jnp.int32)[:, None]
    source = jnp.min(jnp.where(place, order[None, :], slots), axis=1)
    source_row = jnp.sum(jnp.where(place, local_row[None, :], 0), axis=1)
    source_col = jnp.sum(jnp.where(place, local_col[None, :], 0), axis=1)

    dims = (
        rows, cols, slots, size, tiles_row, tiles_col, cap, chunk, feat_chunk, coarse_nodes,
    )
    smem = pl.BlockSpec(memory_space=pltpu.SMEM)
    vmem = pl.BlockSpec(memory_space=pltpu.VMEM)
    hbm = pl.BlockSpec(memory_space=pl.ANY)
    dma = pltpu.SemaphoreType.DMA
    coarse_features, arrived = pl.pallas_call(
        functools.partial(kernel, dims),
        out_shape=(
            jax.ShapeDtypeStruct((tiles_row, half, feat_width), BF16),
            jax.ShapeDtypeStruct((devices * cap, half, half), BF16),
        ),
        in_specs=[smem] * 6 + [vmem] * 5 + [hbm],
        out_specs=(vmem, hbm),
        scratch_shapes=[
            pltpu.VMEM((tiles_row, size, size), BF16),
            pltpu.VMEM((tiles_col, size, size), BF16),
            pltpu.VMEM((2, chunk, size, size), BF16),
            pltpu.VMEM((slots, half, size), BF16),
            pltpu.VMEM((LAG + 1, chunk, half, size), BF16),
            pltpu.VMEM((slots, half, size), BF16),
            pltpu.VMEM((slots, half, half), BF16),
            pltpu.VMEM((slots, half, half), BF16),
            pltpu.VMEM((slots + 1, half, half), F32),
            pltpu.VMEM((tiles_row, half, feat_width), BF16),
            pltpu.VMEM((tiles_row, half, feat_width), BF16),
            pltpu.VMEM((tiles_row, half, feat_width), BF16),
            pltpu.VMEM((half, 128), F32),
            pltpu.VMEM((devices, tiles_row, half), F32),
            pltpu.VMEM((tiles_row, half, half), F32),
            pltpu.VMEM((tiles_row, 1, half), F32),
            pltpu.VMEM((devices * cap, half, half), BF16),
            dma((2,)),
            dma((chunks,)), dma((chunks,)), dma((chunks,)), dma((chunks,)),
            dma((feat_chunks,)), dma((feat_chunks,)),
            dma((devices,)), dma((devices,)), dma((devices,)), dma((devices,)),
            dma(()),
        ],
        compiler_params=pltpu.CompilerParams(
            collective_id=0, has_side_effects=True, vmem_limit_bytes=58 * 2**20
        ),
    )(
        local_row, local_col, pert_id, source, source_row, source_col,
        row_tab, col_tab, pert_sum, join_weight,
        features.reshape(tiles_row, size, feat_width), tile_values,
    )
    return coarse_features.reshape(tiles_row * half, feat_width), arrived


def solution(mesh):
    placed = (
        P("row", None),
        P(),
        P(),
        P(("row", "col")),
        P(("row", "col"), None, None),
        P(("row", "col")),
        P(("row", "col"), None, None),
        P(("row", "col"), None),
    )
    return jax.shard_map(
        local,
        mesh=mesh,
        in_specs=placed,
        out_specs=(P("row", None), P(("row", "col"), None, None)),
        check_vma=False,
    )
```

```python
import functools

import jax
import jax.numpy as jnp
from jax import lax
from jax.experimental import pallas as pl
from jax.experimental.pallas import tpu as pltpu
from jax.sharding import PartitionSpec as P

F32 = jnp.float32
BF16 = jnp.bfloat16
LAG = 3


def onehot(table_row, size):
    levels = lax.broadcasted_iota(jnp.int32, (size, size), 0)
    return (table_row == levels).astype(F32).astype(BF16)


def kernel(
    dims,
    tile_id, pert_slot, source, pair_tab, pert_in, weight, feats, tiles,
    feat_out, quarter_out,
    row_hot, col_hot, pert, inbox, row_send, row_keep, row_recv, col_send, col_recv, quarter,
    feat_send, feat_keep, feat_recv, total, deg_recv, row_scale, col_scale, out_send,
    in_sem, row_ss, row_rs, col_ss, col_rs, feat_ss, feat_rs, deg_ss, deg_rs, out_ss, out_rs,
    own_sem,
):
    (
        rows, cols, slots, size, tiles_row, tiles_col, cap, chunk, feat_chunk, coarse_nodes,
        pert_count,
    ) = dims
    half = size // 2
    devices = rows * cols
    chunks = slots // chunk
    feat_chunks = tiles_row // feat_chunk
    r = lax.axis_index("row")
    c = lax.axis_index("col")
    me = r * cols + c
    row_peer = (lax.rem(r + rows // 2, rows), c)
    col_peer = (r, lax.rem(c + cols // 2, cols))

    def fetch(k):
        return pltpu.make_async_copy(
            tiles.at[pl.ds(k * chunk, chunk)], inbox.at[lax.rem(k, 2)], in_sem.at[lax.rem(k, 2)]
        )

    def row_copy(k):
        part = pl.ds(k * chunk, chunk)
        return pltpu.make_async_remote_copy(
            src_ref=row_send.at[part], dst_ref=row_recv.at[part],
            send_sem=row_ss.at[k], recv_sem=row_rs.at[k],
            device_id=row_peer, device_id_type=pl.DeviceIdType.MESH,
        )

    def col_copy(k):
        part = pl.ds(k * chunk, chunk)
        return pltpu.make_async_remote_copy(
            src_ref=col_send.at[part], dst_ref=col_recv.at[part],
            send_sem=col_ss.at[k], recv_sem=col_rs.at[k],
            device_id=col_peer, device_id_type=pl.DeviceIdType.MESH,
        )

    def feat_copy(k):
        part = pl.ds(k * feat_chunk, feat_chunk)
        return pltpu.make_async_remote_copy(
            src_ref=feat_send.at[part], dst_ref=feat_recv.at[part],
            send_sem=feat_ss.at[k], recv_sem=feat_rs.at[k],
            device_id=row_peer, device_id_type=pl.DeviceIdType.MESH,
        )

    def deg_copy(peer, slot):
        return pltpu.make_async_remote_copy(
            src_ref=deg_recv.at[me], dst_ref=deg_recv.at[slot],
            send_sem=deg_ss.at[peer], recv_sem=deg_rs.at[slot],
            device_id=(peer // cols, lax.rem(peer, cols)),
            device_id_type=pl.DeviceIdType.MESH,
        )

    def out_copy(peer, slot):
        return pltpu.make_async_remote_copy(
            src_ref=out_send.at[pl.ds(peer * cap, cap)],
            dst_ref=quarter_out.at[pl.ds(slot * cap, cap)],
            send_sem=out_ss.at[peer], recv_sem=out_rs.at[slot],
            device_id=(peer // cols, lax.rem(peer, cols)),
            device_id_type=pl.DeviceIdType.MESH,
        )

    def over_peers(body):
        def step(k, carry):
            body(lax.rem(me + k, devices))
            return carry

        lax.fori_loop(1, devices, step, 0)

    fetch(0).start()
    barrier = pltpu.get_barrier_semaphore()

    def greet(peer):
        pl.semaphore_signal(
            barrier, inc=1, device_id=(peer // cols, lax.rem(peer, cols)),
            device_id_type=pl.DeviceIdType.MESH,
        )

    over_peers(greet)

    def build(hot, first, count, side):
        def one(i, carry):
            k = first + i
            odd = pair_tab[pl.ds(coarse_nodes // size + k, 1)] - k * size
            even = lax.broadcasted_iota(jnp.int32, (1, size), 1)
            slot = jnp.where(side == 1, odd, even)
            hot[i] = onehot(slot ^ (half * (1 - side)), size)
            return carry

        lax.fori_loop(0, count, one, 0)

    row_first = lax.rem(r, rows // 2) * tiles_row
    col_begin = lax.rem(c, cols // 2) * tiles_col
    build(row_hot, row_first, tiles_row, r // (rows // 2))
    build(col_hot, col_begin, tiles_col, c // (cols // 2))
    for p in range(pert_count):
        value = jnp.zeros((size, size), F32)
        for q in range(pert_count):
            share = jnp.where(pert_slot[p] == pert_slot[q], 1.0, 0.0)
            value = value + pert_in[q].astype(F32) * share
        pert[p] = value
    pert[pert_count] = jnp.zeros((size, size), F32)
    total[...] = jnp.zeros_like(total)
    quarter[slots] = jnp.zeros((half, half), F32)
    pl.semaphore_wait(barrier, devices - 1)

    def pair_tiles(k):
        @pl.when(k + 1 < chunks)
        def _():
            fetch(k + 1).start()

        fetch(k).wait()
        box = lax.rem(k, 2)
        keep = lax.rem(k, LAG + 1)
        for t in range(chunk):
            n = k * chunk + t
            extra = jnp.int32(pert_count)
            for p in range(pert_count):
                extra = jnp.where(pert_slot[p] == n, p, extra)
            tile = (inbox[box, t].astype(F32) + pert[extra]).astype(BF16)
            paired = jnp.dot(
                row_hot[tile_id[n] // tiles_col], tile, preferred_element_type=F32
            ).astype(BF16)
            paired = lax.dot_general(
                paired, col_hot[tile_id[n] % tiles_col], (((1,), (1,)), ((), ())),
                preferred_element_type=F32,
            ).astype(BF16)
            row_send[n] = paired[:half]
            row_keep[keep, t] = paired[half:]
        row_copy(k).start()

    def pair_feats(k):
        def one(t, carry):
            n = k * feat_chunk + t
            paired = jnp.dot(row_hot[n], feats[n], preferred_element_type=F32).astype(BF16)
            feat_send[n] = paired[:half]
            feat_keep[n] = paired[half:]
            return carry

        lax.fori_loop(0, feat_chunk, one, 0)

    def sum_rows(k):
        row_copy(k).wait_recv()
        keep = lax.rem(k, LAG + 1)
        for t in range(chunk):
            n = k * chunk + t
            summed = row_keep[keep, t].astype(F32) + row_recv[n].astype(F32)
            col_send[n] = summed[:, :half].astype(BF16)
            quarter[n] = summed[:, half:]
        col_copy(k).start()

    def sum_cols(k):
        col_copy(k).wait_recv()
        lanes = lax.broadcasted_iota(jnp.int32, (half, 128), 1)
        for t in range(chunk):
            n = k * chunk + t
            value = quarter[n] + col_recv[n].astype(F32)
            quarter[n] = value
            sums = jnp.sum(value, axis=1, keepdims=True)
            total[...] += jnp.where(lanes == tile_id[n] // tiles_col, sums, 0.0)

    def step(k, carry):
        pl.when(k < chunks)(lambda: pair_tiles(k))
        pl.when((k >= chunks) & (k < chunks + feat_chunks))(lambda: pair_feats(k - chunks))
        pl.when((k >= LAG) & (k < chunks + LAG))(lambda: sum_rows(k - LAG))
        pl.when((k >= 2 * LAG) & (k < chunks + 2 * LAG))(lambda: sum_cols(k - 2 * LAG))
        return carry

    lax.fori_loop(0, chunks + max(2 * LAG, feat_chunks), step, 0)

    deg_recv[me] = total[...].T[:tiles_row]
    over_peers(lambda peer: deg_copy(peer, me).start())
    over_peers(lambda peer: deg_copy(peer, peer).wait_recv())

    def inverse_root(row):
        def add(j, value):
            return value + deg_recv[row * cols + j]

        sums = lax.fori_loop(0, cols, add, jnp.zeros((tiles_row, half), F32))
        return 1.0 / jnp.sqrt(1.0 + sums / coarse_nodes)

    col_owner = c // (cols // 2) * (rows // 2) + col_begin // tiles_row
    col_first = lax.rem(col_begin, tiles_row)
    col_root = inverse_root(col_owner)
    row_root = inverse_root(r)
    row_root = jnp.concatenate([row_root, jnp.zeros((128 - tiles_row, half), F32)], axis=0).T
    for i in range(tiles_row):
        col_scale[i] = col_root[i : i + 1]
        row_scale[i] = jnp.broadcast_to(row_root[:, i : i + 1], (half, half))

    def fill(peer):
        for m in range(cap):
            t = peer * cap + m
            n = source[t]
            place = tile_id[jnp.minimum(n, slots - 1)]
            value = (
                quarter[n] * row_scale[place // tiles_col]
            ) * col_scale[place % tiles_col + col_first]
            out_send[t] = value.astype(BF16)

    stride = devices // feat_chunks

    def send(k, carry):
        peer = lax.rem(me + k, devices)
        fill(peer)
        out_copy(peer, me).start()
        pl.when(lax.rem(k, stride) == 1)(lambda: feat_copy(k // stride).start())
        return carry

    lax.fori_loop(1, devices, send, 0)
    fill(me)
    own = pltpu.make_async_copy(
        out_send.at[pl.ds(me * cap, cap)], quarter_out.at[pl.ds(me * cap, cap)], own_sem
    )
    own.start()

    def join(k, carry):
        feat_copy(k).wait_recv()

        def one(t, inner):
            n = k * feat_chunk + t
            merged = (feat_keep[n].astype(F32) + feat_recv[n].astype(F32)).astype(BF16)
            joined = jnp.dot(merged, weight[...], preferred_element_type=F32)
            feat_out[n] = (joined * row_scale[n][:, :1]).astype(BF16)
            return inner

        return lax.fori_loop(0, feat_chunk, one, carry)

    lax.fori_loop(0, feat_chunks, join, 0)

    def finish_pair(k, carry):
        row_copy(k).wait_send()
        col_copy(k).wait_send()
        return carry

    def finish_feat(k, carry):
        feat_copy(k).wait_send()
        return carry

    lax.fori_loop(0, chunks, finish_pair, 0)
    lax.fori_loop(0, feat_chunks, finish_feat, 0)
    over_peers(lambda peer: deg_copy(peer, me).wait_send())
    own.wait()
    over_peers(lambda peer: out_copy(peer, me).wait_send())
    over_peers(lambda peer: out_copy(peer, peer).wait_recv())


def hand_over(*values):
    parts = 8

    def body(*refs):
        for i in range(len(values)):
            refs[len(values) + i][...] = refs[i][...]

    specs = [
        pl.BlockSpec(
            (value.shape[0] // parts,) + value.shape[1:],
            functools.partial(lambda rank, i: (i,) + (0,) * rank, value.ndim - 1),
        )
        for value in values
    ]
    return pl.pallas_call(
        body,
        grid=(parts,),
        out_shape=tuple(jax.ShapeDtypeStruct(value.shape, value.dtype) for value in values),
        in_specs=specs,
        out_specs=tuple(specs),
        compiler_params=pltpu.CompilerParams(vmem_limit_bytes=58 * 2**20),
    )(*values)


def local(features, join_weight, partner, tile_index, tile_values, pert_slot, pert_values, routes):
    rows = lax.axis_size("row")
    cols = lax.axis_size("col")
    slots, size, _ = tile_values.shape
    half = size // 2
    feat_width = features.shape[1]
    tiles_row = features.shape[0] // size
    node_tiles = partner.shape[0] // size
    tiles_col = node_tiles // cols
    coarse_count = node_tiles // 2
    coarse_nodes = coarse_count * size
    cap = routes.shape[1]
    pert_count = pert_slot.shape[0]
    devices = rows * cols
    chunk = next(n for n in (4, 2, 1) if slots % n == 0)
    feat_chunk = next(n for n in (4, 2, 1) if tiles_row % n == 0)
    chunks = slots // chunk
    feat_chunks = tiles_row // feat_chunk

    order = jnp.arange(slots, dtype=jnp.int32)
    targets = routes[:, 0]
    earlier = jnp.sum(
        ((targets[:, None] == targets[None, :]) & (order[None, :] < order[:, None])).astype(
            jnp.int32
        ),
        axis=1,
    )
    position = targets * cap + earlier
    place = position[None, :] == jnp.arange(devices * cap, dtype=jnp.int32)[:, None]
    source = jnp.min(jnp.where(place, order[None, :], slots), axis=1)

    dims = (
        rows, cols, slots, size, tiles_row, tiles_col, cap, chunk, feat_chunk, coarse_nodes,
        pert_count,
    )
    smem = pl.BlockSpec(memory_space=pltpu.SMEM)
    vmem = pl.BlockSpec(memory_space=pltpu.VMEM)
    hbm = pl.BlockSpec(memory_space=pl.ANY)
    dma = pltpu.SemaphoreType.DMA
    coarse_features, arrived = pl.pallas_call(
        functools.partial(kernel, dims),
        out_shape=(
            jax.ShapeDtypeStruct((tiles_row, half, feat_width), BF16),
            jax.ShapeDtypeStruct((devices * cap, half, half), BF16),
        ),
        in_specs=[smem] * 3 + [vmem] * 4 + [hbm],
        out_specs=(vmem, hbm),
        scratch_shapes=[
            pltpu.VMEM((tiles_row, size, size), BF16),
            pltpu.VMEM((tiles_col, size, size), BF16),
            pltpu.VMEM((pert_count + 1, size, size), F32),
            pltpu.VMEM((2, chunk, size, size), BF16),
            pltpu.VMEM((slots, half, size), BF16),
            pltpu.VMEM((LAG + 1, chunk, half, size), BF16),
            pltpu.VMEM((slots, half, size), BF16),
            pltpu.VMEM((slots, half, half), BF16),
            pltpu.VMEM((slots, half, half), BF16),
            pltpu.VMEM((slots + 1, half, half), F32),
            pltpu.VMEM((tiles_row, half, feat_width), BF16),
            pltpu.VMEM((tiles_row, half, feat_width), BF16),
            pltpu.VMEM((tiles_row, half, feat_width), BF16),
            pltpu.VMEM((half, 128), F32),
            pltpu.VMEM((devices, tiles_row, half), F32),
            pltpu.VMEM((tiles_row, half, half), F32),
            pltpu.VMEM((tiles_row, 1, half), F32),
            pltpu.VMEM((devices * cap, half, half), BF16),
            dma((2,)),
            dma((chunks,)), dma((chunks,)), dma((chunks,)), dma((chunks,)),
            dma((feat_chunks,)), dma((feat_chunks,)),
            dma((devices,)), dma((devices,)), dma((devices,)), dma((devices,)),
            dma(()),
        ],
        compiler_params=pltpu.CompilerParams(
            collective_id=0, has_side_effects=True, vmem_limit_bytes=58 * 2**20
        ),
    )(
        tile_index, pert_slot, source, partner.reshape(node_tiles, size), pert_values, join_weight,
        features.reshape(tiles_row, size, feat_width), tile_values,
    )
    coarse_features, arrived = hand_over(
        coarse_features.reshape(tiles_row * half, feat_width), arrived
    )
    return coarse_features, arrived


def solution(mesh):
    placed = (
        P("row", None),
        P(),
        P(),
        P(("row", "col")),
        P(("row", "col"), None, None),
        P(("row", "col")),
        P(("row", "col"), None, None),
        P(("row", "col"), None),
    )
    return jax.shard_map(
        local,
        mesh=mesh,
        in_specs=placed,
        out_specs=(P("row", None), P(("row", "col"), None, None)),
        check_vma=False,
    )
```

```python
import functools

import jax
import jax.numpy as jnp
from jax import lax
from jax.experimental import pallas as pl
from jax.experimental.pallas import tpu as pltpu
from jax.sharding import PartitionSpec as P

F32 = jnp.float32
BF16 = jnp.bfloat16
LAG = 3


def onehot(table_row, size):
    levels = lax.broadcasted_iota(jnp.int32, (size, size), 0)
    return (table_row == levels).astype(F32).astype(BF16)


def kernel(
    dims,
    tile_id, pert_slot, source, pair_tab, pert_in, weight, feats, tiles,
    feat_out, quarter_out,
    row_hot, col_hot, pert, inbox, row_send, row_keep, row_recv, col_send, col_recv, quarter,
    feat_send, feat_keep, feat_recv, total, deg_recv, row_scale, col_scale, out_send,
    in_sem, row_ss, row_rs, col_ss, col_rs, feat_ss, feat_rs, deg_ss, deg_rs, out_ss, out_rs,
    own_sem,
):
    (
        rows, cols, slots, size, tiles_row, tiles_col, cap, chunk, feat_chunk, coarse_nodes,
        pert_count,
    ) = dims
    half = size // 2
    devices = rows * cols
    chunks = slots // chunk
    feat_chunks = tiles_row // feat_chunk
    r = lax.axis_index("row")
    c = lax.axis_index("col")
    me = r * cols + c
    row_peer = (lax.rem(r + rows // 2, rows), c)
    col_peer = (r, lax.rem(c + cols // 2, cols))

    def fetch(k):
        return pltpu.make_async_copy(
            tiles.at[pl.ds(k * chunk, chunk)], inbox.at[lax.rem(k, 2)], in_sem.at[lax.rem(k, 2)]
        )

    def row_copy(k):
        part = pl.ds(k * chunk, chunk)
        return pltpu.make_async_remote_copy(
            src_ref=row_send.at[part], dst_ref=row_recv.at[part],
            send_sem=row_ss.at[k], recv_sem=row_rs.at[k],
            device_id=row_peer, device_id_type=pl.DeviceIdType.MESH,
        )

    def col_copy(k):
        part = pl.ds(k * chunk, chunk)
        return pltpu.make_async_remote_copy(
            src_ref=col_send.at[part], dst_ref=col_recv.at[part],
            send_sem=col_ss.at[k], recv_sem=col_rs.at[k],
            device_id=col_peer, device_id_type=pl.DeviceIdType.MESH,
        )

    def feat_copy(k):
        part = pl.ds(k * feat_chunk, feat_chunk)
        return pltpu.make_async_remote_copy(
            src_ref=feat_send.at[part], dst_ref=feat_recv.at[part],
            send_sem=feat_ss.at[k], recv_sem=feat_rs.at[k],
            device_id=row_peer, device_id_type=pl.DeviceIdType.MESH,
        )

    def deg_copy(peer, slot):
        return pltpu.make_async_remote_copy(
            src_ref=deg_recv.at[me], dst_ref=deg_recv.at[slot],
            send_sem=deg_ss.at[peer], recv_sem=deg_rs.at[slot],
            device_id=(peer // cols, lax.rem(peer, cols)),
            device_id_type=pl.DeviceIdType.MESH,
        )

    def out_copy(peer, slot):
        return pltpu.make_async_remote_copy(
            src_ref=out_send.at[pl.ds(peer * cap, cap)],
            dst_ref=quarter_out.at[pl.ds(slot * cap, cap)],
            send_sem=out_ss.at[peer], recv_sem=out_rs.at[slot],
            device_id=(peer // cols, lax.rem(peer, cols)),
            device_id_type=pl.DeviceIdType.MESH,
        )

    def over_peers(body):
        def step(k, carry):
            body(lax.rem(me + k, devices))
            return carry

        lax.fori_loop(1, devices, step, 0)

    fetch(0).start()
    barrier = pltpu.get_barrier_semaphore()

    def greet(peer):
        pl.semaphore_signal(
            barrier, inc=1, device_id=(peer // cols, lax.rem(peer, cols)),
            device_id_type=pl.DeviceIdType.MESH,
        )

    over_peers(greet)

    def build(hot, first, count, side):
        def one(i, carry):
            k = first + i
            odd = pair_tab[pl.ds(coarse_nodes // size + k, 1)] - k * size
            even = lax.broadcasted_iota(jnp.int32, (1, size), 1)
            slot = jnp.where(side == 1, odd, even)
            hot[i] = onehot(slot ^ (half * (1 - side)), size)
            return carry

        lax.fori_loop(0, count, one, 0)

    row_first = lax.rem(r, rows // 2) * tiles_row
    col_begin = lax.rem(c, cols // 2) * tiles_col
    build(row_hot, row_first, tiles_row, r // (rows // 2))
    build(col_hot, col_begin, tiles_col, c // (cols // 2))
    for p in range(pert_count):
        value = jnp.zeros((size, size), F32)
        for q in range(pert_count):
            share = jnp.where(pert_slot[p] == pert_slot[q], 1.0, 0.0)
            value = value + pert_in[q].astype(F32) * share
        pert[p] = value
    pert[pert_count] = jnp.zeros((size, size), F32)
    total[...] = jnp.zeros_like(total)
    quarter[slots] = jnp.zeros((half, half), F32)
    pl.semaphore_wait(barrier, devices - 1)

    def pair_tiles(k):
        @pl.when(k + 1 < chunks)
        def _():
            fetch(k + 1).start()

        fetch(k).wait()
        box = lax.rem(k, 2)
        keep = lax.rem(k, LAG + 1)
        for t in range(chunk):
            n = k * chunk + t
            extra = jnp.int32(pert_count)
            for p in range(pert_count):
                extra = jnp.where(pert_slot[p] == n, p, extra)
            tile = (inbox[box, t].astype(F32) + pert[extra]).astype(BF16)
            paired = jnp.dot(
                row_hot[tile_id[n] // tiles_col], tile, preferred_element_type=F32
            ).astype(BF16)
            paired = lax.dot_general(
                paired, col_hot[tile_id[n] % tiles_col], (((1,), (1,)), ((), ())),
                preferred_element_type=F32,
            ).astype(BF16)
            row_send[n] = paired[:half]
            row_keep[keep, t] = paired[half:]
        row_copy(k).start()

    def pair_feats(k):
        def one(t, carry):
            n = k * feat_chunk + t
            paired = jnp.dot(row_hot[n], feats[n], preferred_element_type=F32).astype(BF16)
            feat_send[n] = paired[:half]
            feat_keep[n] = paired[half:]
            return carry

        lax.fori_loop(0, feat_chunk, one, 0)

    def sum_rows(k):
        row_copy(k).wait_recv()
        keep = lax.rem(k, LAG + 1)
        for t in range(chunk):
            n = k * chunk + t
            summed = row_keep[keep, t].astype(F32) + row_recv[n].astype(F32)
            col_send[n] = summed[:, :half].astype(BF16)
            quarter[n] = summed[:, half:]
        col_copy(k).start()

    def sum_cols(k):
        col_copy(k).wait_recv()
        lanes = lax.broadcasted_iota(jnp.int32, (half, 128), 1)
        for t in range(chunk):
            n = k * chunk + t
            value = quarter[n] + col_recv[n].astype(F32)
            quarter[n] = value
            sums = jnp.sum(value, axis=1, keepdims=True)
            total[...] += jnp.where(lanes == tile_id[n] // tiles_col, sums, 0.0)

    def step(k, carry):
        pl.when(k < chunks)(lambda: pair_tiles(k))
        pl.when((k >= chunks) & (k < chunks + feat_chunks))(lambda: pair_feats(k - chunks))
        pl.when((k >= LAG) & (k < chunks + LAG))(lambda: sum_rows(k - LAG))
        pl.when((k >= 2 * LAG) & (k < chunks + 2 * LAG))(lambda: sum_cols(k - 2 * LAG))
        return carry

    lax.fori_loop(0, chunks + max(2 * LAG, feat_chunks), step, 0)

    deg_recv[me] = total[...].T[:tiles_row]
    over_peers(lambda peer: deg_copy(peer, me).start())
    over_peers(lambda peer: deg_copy(peer, peer).wait_recv())

    def inverse_root(row):
        def add(j, value):
            return value + deg_recv[row * cols + j]

        sums = lax.fori_loop(0, cols, add, jnp.zeros((tiles_row, half), F32))
        return 1.0 / jnp.sqrt(1.0 + sums / coarse_nodes)

    col_owner = c // (cols // 2) * (rows // 2) + col_begin // tiles_row
    col_first = lax.rem(col_begin, tiles_row)
    col_root = inverse_root(col_owner)
    row_root = inverse_root(r)
    row_root = jnp.concatenate([row_root, jnp.zeros((128 - tiles_row, half), F32)], axis=0).T
    for i in range(tiles_row):
        col_scale[i] = col_root[i : i + 1]
        row_scale[i] = jnp.broadcast_to(row_root[:, i : i + 1], (half, half))

    def fill(peer):
        for m in range(cap):
            t = peer * cap + m
            n = source[t]
            place = tile_id[jnp.minimum(n, slots - 1)]
            value = (
                quarter[n] * row_scale[place // tiles_col]
            ) * col_scale[place % tiles_col + col_first]
            out_send[t] = value.astype(BF16)

    stride = devices // feat_chunks

    def send(k, carry):
        peer = lax.rem(me + k, devices)
        fill(peer)
        out_copy(peer, me).start()
        pl.when(lax.rem(k, stride) == 1)(lambda: feat_copy(k // stride).start())
        return carry

    lax.fori_loop(1, devices, send, 0)
    fill(me)
    own = pltpu.make_async_copy(
        out_send.at[pl.ds(me * cap, cap)], quarter_out.at[pl.ds(me * cap, cap)], own_sem
    )
    own.start()

    def join(k, carry):
        feat_copy(k).wait_recv()

        def one(t, inner):
            n = k * feat_chunk + t
            merged = (feat_keep[n].astype(F32) + feat_recv[n].astype(F32)).astype(BF16)
            joined = jnp.dot(merged, weight[...], preferred_element_type=F32)
            feat_out[n] = (joined * row_scale[n][:, :1]).astype(BF16)
            return inner

        return lax.fori_loop(0, feat_chunk, one, carry)

    lax.fori_loop(0, feat_chunks, join, 0)

    def finish_pair(k, carry):
        row_copy(k).wait_send()
        col_copy(k).wait_send()
        return carry

    def finish_feat(k, carry):
        feat_copy(k).wait_send()
        return carry

    lax.fori_loop(0, chunks, finish_pair, 0)
    lax.fori_loop(0, feat_chunks, finish_feat, 0)
    over_peers(lambda peer: deg_copy(peer, me).wait_send())
    own.wait()
    over_peers(lambda peer: out_copy(peer, me).wait_send())
    over_peers(lambda peer: out_copy(peer, peer).wait_recv())


def hand_over(*values):
    parts = 8

    def body(*refs):
        for i in range(len(values)):
            refs[len(values) + i][...] = refs[i][...]

    specs = [
        pl.BlockSpec(
            (value.shape[0] // parts,) + value.shape[1:],
            functools.partial(lambda rank, i: (i,) + (0,) * rank, value.ndim - 1),
        )
        for value in values
    ]
    return pl.pallas_call(
        body,
        grid=(parts,),
        out_shape=tuple(jax.ShapeDtypeStruct(value.shape, value.dtype) for value in values),
        in_specs=specs,
        out_specs=tuple(specs),
        compiler_params=pltpu.CompilerParams(vmem_limit_bytes=58 * 2**20),
    )(*values)


def local(features, join_weight, partner, tile_index, tile_values, pert_slot, pert_values, routes):
    rows = lax.axis_size("row")
    cols = lax.axis_size("col")
    slots, size, _ = tile_values.shape
    half = size // 2
    feat_width = features.shape[1]
    tiles_row = features.shape[0] // size
    node_tiles = partner.shape[0] // size
    tiles_col = node_tiles // cols
    coarse_count = node_tiles // 2
    coarse_nodes = coarse_count * size
    cap = routes.shape[1]
    pert_count = pert_slot.shape[0]
    devices = rows * cols
    chunk = next(n for n in (2, 1) if slots % n == 0)
    feat_chunk = next(n for n in (4, 2, 1) if tiles_row % n == 0)
    chunks = slots // chunk
    feat_chunks = tiles_row // feat_chunk

    order = jnp.arange(slots, dtype=jnp.int32)
    targets = routes[:, 0]
    earlier = jnp.sum(
        ((targets[:, None] == targets[None, :]) & (order[None, :] < order[:, None])).astype(
            jnp.int32
        ),
        axis=1,
    )
    position = targets * cap + earlier
    place = position[None, :] == jnp.arange(devices * cap, dtype=jnp.int32)[:, None]
    source = jnp.min(jnp.where(place, order[None, :], slots), axis=1)

    dims = (
        rows, cols, slots, size, tiles_row, tiles_col, cap, chunk, feat_chunk, coarse_nodes,
        pert_count,
    )
    smem = pl.BlockSpec(memory_space=pltpu.SMEM)
    vmem = pl.BlockSpec(memory_space=pltpu.VMEM)
    hbm = pl.BlockSpec(memory_space=pl.ANY)
    dma = pltpu.SemaphoreType.DMA
    coarse_features, arrived = pl.pallas_call(
        functools.partial(kernel, dims),
        out_shape=(
            jax.ShapeDtypeStruct((tiles_row, half, feat_width), BF16),
            jax.ShapeDtypeStruct((devices * cap, half, half), BF16),
        ),
        in_specs=[smem] * 3 + [vmem] * 4 + [hbm],
        out_specs=(vmem, hbm),
        scratch_shapes=[
            pltpu.VMEM((tiles_row, size, size), BF16),
            pltpu.VMEM((tiles_col, size, size), BF16),
            pltpu.VMEM((pert_count + 1, size, size), F32),
            pltpu.VMEM((2, chunk, size, size), BF16),
            pltpu.VMEM((slots, half, size), BF16),
            pltpu.VMEM((LAG + 1, chunk, half, size), BF16),
            pltpu.VMEM((slots, half, size), BF16),
            pltpu.VMEM((slots, half, half), BF16),
            pltpu.VMEM((slots, half, half), BF16),
            pltpu.VMEM((slots + 1, half, half), F32),
            pltpu.VMEM((tiles_row, half, feat_width), BF16),
            pltpu.VMEM((tiles_row, half, feat_width), BF16),
            pltpu.VMEM((tiles_row, half, feat_width), BF16),
            pltpu.VMEM((half, 128), F32),
            pltpu.VMEM((devices, tiles_row, half), F32),
            pltpu.VMEM((tiles_row, half, half), F32),
            pltpu.VMEM((tiles_row, 1, half), F32),
            pltpu.VMEM((devices * cap, half, half), BF16),
            dma((2,)),
            dma((chunks,)), dma((chunks,)), dma((chunks,)), dma((chunks,)),
            dma((feat_chunks,)), dma((feat_chunks,)),
            dma((devices,)), dma((devices,)), dma((devices,)), dma((devices,)),
            dma(()),
        ],
        compiler_params=pltpu.CompilerParams(
            collective_id=0, has_side_effects=True, vmem_limit_bytes=58 * 2**20
        ),
    )(
        tile_index, pert_slot, source, partner.reshape(node_tiles, size), pert_values, join_weight,
        features.reshape(tiles_row, size, feat_width), tile_values,
    )
    coarse_features, arrived = hand_over(
        coarse_features.reshape(tiles_row * half, feat_width), arrived
    )
    return coarse_features, arrived


def solution(mesh):
    placed = (
        P("row", None),
        P(),
        P(),
        P(("row", "col")),
        P(("row", "col"), None, None),
        P(("row", "col")),
        P(("row", "col"), None, None),
        P(("row", "col"), None),
    )
    return jax.shard_map(
        local,
        mesh=mesh,
        in_specs=placed,
        out_specs=(P("row", None), P(("row", "col"), None, None)),
        check_vma=False,
    )
```
